32 devices in a mesh: dp: 4 (over y, x), rows: 8 (over z, core).
Axes of the slice: x: 2, y: 2, z: 4, core: 2. Of those that a mesh axis runs over, the one named last changes fastest.
Arguments:
- scenes: bfloat16 [4, 256, 256, 384], P('dp', 'rows'), may hold values from -6 to 6
- prompt: bfloat16 [256, 256, 384], P('rows'), may hold values from -6 to 6
- cotangent: bfloat16 [4, 256, 256, 384], P('dp', 'rows'), may hold values from -6 to 6
- first_weight: bfloat16 [2, 8, 48, 48], replicated, may hold values from -0.625 to 0.625
- first_bias: float32 [2, 384], replicated, may hold values from -3 to 3
- second_weight: bfloat16 [2, 8, 48, 48], replicated, may hold values from -0.625 to 0.625
- second_bias: float32 [2, 384], replicated, may hold values from -3 to 3
Outputs:
- mixed: bfloat16 [4, 256, 256, 384], P('dp', 'rows')
- prompt_grad: float32 [256, 256, 384], P('rows', 'dp')
The draws below stay inside these ranges and needn't reach their ends.
All inputs are finite; a program needn't handle non-finite values.
Results may differ from the reference program's by a relative error of at most 0.014.
Values may be sent and summed in bfloat16 or wider, within the bound.
A program may use at most 128 MiB of HBM per device.

```python
import math
import jax
import jax.numpy as jnp
from jax import lax

H = 256
W = 256
C = 384
NB = 8
BS = 48
KW = 128
SCENES = 4
N_DP = 4


def raised(drawn, key, source, target, shards_of, factor):
    def block_of(position):
        return (jnp.arange(drawn.shape[position]) // (drawn.shape[position] // shards_of)).reshape((-1,) + (1,) * (drawn.ndim - 1 - position))

    near = jax.random.permutation(key, shards_of)[block_of(target)]
    far = (block_of(target) + shards_of // 2) % shards_of
    return jnp.where((block_of(source) == near) | (block_of(source) == far), factor * drawn, drawn)


def block_levels(key, shape, cuts, smallest, top_value):
    level = 1.0
    for dim, shards_of in cuts:
        heights = jax.random.uniform(jax.random.fold_in(jax.random.fold_in(key, 6), dim), (shards_of,), jnp.float32, smallest / len(cuts), top_value / len(cuts))
        level = level * jnp.repeat(jnp.exp(heights), shape[dim] // shards_of).reshape((-1,) + (1,) * (len(shape) - 1 - dim))
    return level


def scatter_about(key, extent, width, reach, cuts=(), kind=jnp.bfloat16):
    loudness = block_levels(key, extent, cuts, -0.22, 0.18) if cuts else 1.0
    result = jax.random.normal(key, extent, jnp.float32) * width * loudness
    return jnp.minimum(jnp.maximum(result, -reach), reach).astype(kind)


def gaussian_with(rng, shape, width, bound, cuts, heavy, kind=jnp.bfloat16):
    drawn = width * jax.random.normal(rng, shape, jnp.float32)
    if cuts:
        drawn = drawn * block_levels(rng, shape, cuts, -0.22, 0.18)
    return jnp.clip(raised(drawn, jax.random.fold_in(rng, 3), *heavy), -bound, bound).astype(kind)


def setup_inputs(seed: int = 0) -> dict:
    keys = jax.random.split(jax.random.key(seed), 8)
    scenes = scatter_about(keys[0], (SCENES, H, W, C), 1.0, 6.0, ((0, 4), (1, 8)))
    prompt = scatter_about(keys[1], (H, W, C), 1.0, 6.0, ((0, 8),))
    cotangent = gaussian_with(keys[2], (SCENES, H, W, C), 1.0, 6.0, ((0, 4), (1, 8)), (0, 2, 4, 2.0))
    first_weight = scatter_about(keys[3], (2, NB, BS, BS), (2 * BS) ** -0.5, 0.625)
    first_bias = scatter_about(keys[4], (2, C), 0.5, 3.0, (), jnp.float32)
    second_weight = scatter_about(keys[5], (2, NB, BS, BS), (2 * BS) ** -0.5, 0.625)
    second_bias = scatter_about(keys[6], (2, C), 0.5, 3.0, (), jnp.float32)
    return dict(scenes=scenes, prompt=prompt, cotangent=cotangent, first_weight=first_weight, first_bias=first_bias, second_weight=second_weight, second_bias=second_bias)


def product(form, left, right):
    return jnp.einsum(form, left.astype(jnp.float32), right.astype(jnp.float32), precision=lax.Precision.HIGHEST)

def row_tables():
    grid_index = jnp.arange(W, dtype=jnp.int32)
    mode_index = jnp.arange(KW, dtype=jnp.int32)
    phases = mode_index[:, None] * grid_index[None, :] % W
    angles = phases.astype(jnp.float32) * (2.0 * math.pi / W)
    factor = 1.0 / math.sqrt(W)
    cosine = jnp.cos(angles) * factor
    sines = jnp.sin(angles) * factor
    forward = jnp.stack([cosine, -sines], axis=0).astype(jnp.bfloat16)
    doubled = jnp.where(mode_index == 0, 1.0, 2.0).astype(jnp.float32)[:, None]
    inverse = jnp.stack([doubled * cosine, -doubled * sines], axis=0).astype(jnp.bfloat16)
    return (forward, jnp.transpose(inverse, (2, 0, 1)))

def column_tables():
    grid_index = jnp.arange(H, dtype=jnp.int32)
    phases = grid_index[:, None] * grid_index[None, :] % H
    angles = phases.astype(jnp.float32) * (2.0 * math.pi / H)
    factor = 1.0 / math.sqrt(H)
    cosine = jnp.cos(angles) * factor
    sines = jnp.sin(angles) * factor
    upper = jnp.stack([cosine, sines], axis=1)
    lower = jnp.stack([-sines, cosine], axis=1)
    forward = jnp.stack([upper, lower], axis=0).astype(jnp.bfloat16)
    return (forward, jnp.transpose(forward, (2, 3, 0, 1)))

def complex_block(weights):
    real_part = weights[0]
    imag_part = weights[1]
    first_row = jnp.stack([real_part, imag_part], axis=2)
    second_row = jnp.stack([-imag_part, real_part], axis=2)
    return jnp.stack([first_row, second_row], axis=0)

def spectral_mix(spectrum, first_block, second_block, first_bias, second_bias):
    layout = spectrum.shape
    pieces = spectrum.reshape(layout[:4] + (NB, BS))
    first_pre = product('smqkbi,qbipj->smpkbj', pieces, first_block) + first_bias.reshape(2, 1, NB, BS)
    hidden = jax.nn.gelu(first_pre, approximate=False).astype(jnp.bfloat16)
    second = product('smqkbi,qbipj->smpkbj', hidden, second_block) + second_bias.reshape(2, 1, NB, BS)
    return (second.astype(jnp.bfloat16).reshape(layout), first_pre)

def spectral_back(back_out, first_pre, first_block, second_block):
    layout = back_out.shape
    pieces = back_out.reshape(layout[:4] + (NB, BS))
    back_hidden = product('smpkbj,qbipj->smqkbi', pieces, second_block)
    cumulative = 0.5 * (1.0 + lax.erf(first_pre * 0.7071067811865476))
    density = jnp.exp(-0.5 * first_pre * first_pre) * 0.3989422804014327
    back_pre = (back_hidden * (cumulative + first_pre * density)).astype(jnp.bfloat16)
    back_spectrum = product('smpkbj,qbipj->smqkbi', back_pre, first_block)
    return back_spectrum.astype(jnp.bfloat16).reshape(layout)

def scene_pass(scene, cotangent, prompt, row_fwd, row_inv, column_fwd, column_inv, first_block, second_block, first_bias, second_bias):
    summed = (scene.astype(jnp.float32) + prompt.astype(jnp.float32)[None]).astype(jnp.bfloat16)
    row_spec = product('pkn,shnc->shpkc', row_fwd, summed).astype(jnp.bfloat16)
    back_spec = product('npk,shnc->shpkc', row_inv, cotangent).astype(jnp.bfloat16)
    spectrum = product('pmqh,shqkc->smpkc', column_fwd, row_spec).astype(jnp.bfloat16)
    output_spec, first_pre = spectral_mix(spectrum, first_block, second_block, first_bias, second_bias)
    grid_spec = product('phqm,smqkc->shpkc', column_inv, output_spec).astype(jnp.bfloat16)
    back_out = product('qhpm,shqkc->smpkc', column_inv, back_spec).astype(jnp.bfloat16)
    back_spectrum = spectral_back(back_out, first_pre, first_block, second_block)
    back_rows = product('pmqh,smpkc->shqkc', column_fwd, back_spectrum).astype(jnp.bfloat16)
    mixed = (summed.astype(jnp.float32) + product('npk,shpkc->shnc', row_inv, grid_spec)).astype(jnp.bfloat16)
    grad_terms = cotangent.astype(jnp.float32) + product('pkn,shpkc->shnc', row_fwd, back_rows)
    return (mixed, grad_terms)

def reference(scenes, prompt, cotangent, first_weight, first_bias, second_weight, second_bias):
    row_fwd, row_inv = row_tables()
    column_fwd, column_inv = column_tables()
    first_block = complex_block(first_weight)
    second_block = complex_block(second_weight)
    group_size = SCENES // N_DP

    def one_scene(partial_value, packed):
        scene, scene_cot = packed
        mixed, grad_terms = scene_pass(scene[None], scene_cot[None], prompt, row_fwd, row_inv, column_fwd, column_inv, first_block, second_block, first_bias, second_bias)
        return (partial_value + grad_terms[0], mixed[0])

    def one_group(totals, packed):
        group_scenes, group_cot = packed
        partial_value, mixed = lax.scan(one_scene, jnp.zeros((H, W, C), jnp.float32), (group_scenes, group_cot))
        rounded = lax.optimization_barrier(partial_value.astype(jnp.bfloat16)).astype(jnp.float32)
        return (totals + rounded, mixed)
    grouped_scenes = scenes.reshape((N_DP, group_size, H, W, C))
    grouped_cot = cotangent.reshape((N_DP, group_size, H, W, C))
    start = jnp.zeros((H, W, C), jnp.float32)
    prompt_grad, mixed = lax.scan(one_group, start, (grouped_scenes, grouped_cot))
    return (mixed.reshape((SCENES, H, W, C)), prompt_grad)
```

```python
import functools
import math

import jax
import jax.numpy as jnp
from jax import lax
from jax.experimental import pallas as pl
from jax.experimental.pallas import tpu as pltpu
from jax.sharding import PartitionSpec as P

VMEM_LIMIT = 48 * 1024 * 1024
HBLOCK = 16


def dot(left, right):
    return jnp.dot(left, right, preferred_element_type=jnp.float32)


def row_tables(width, kept):
    grid_index = jnp.arange(width, dtype=jnp.int32)
    mode_index = jnp.arange(kept, dtype=jnp.int32)
    phases = mode_index[:, None] * grid_index[None, :] % width
    angles = phases.astype(jnp.float32) * (2.0 * math.pi / width)
    factor = 1.0 / math.sqrt(width)
    cosine = jnp.cos(angles) * factor
    sines = jnp.sin(angles) * factor
    forward = jnp.stack([cosine, -sines], axis=0).astype(jnp.bfloat16)
    doubled = jnp.where(mode_index == 0, 1.0, 2.0).astype(jnp.float32)[:, None]
    inverse = jnp.stack([doubled * cosine, -doubled * sines], axis=0).astype(jnp.bfloat16)
    return forward, inverse


def column_tables(height):
    grid_index = jnp.arange(height, dtype=jnp.int32)
    phases = grid_index[:, None] * grid_index[None, :] % height
    angles = phases.astype(jnp.float32) * (2.0 * math.pi / height)
    factor = 1.0 / math.sqrt(height)
    cosine = (jnp.cos(angles) * factor).astype(jnp.bfloat16)
    sines = (jnp.sin(angles) * factor).astype(jnp.bfloat16)
    forward = jnp.block([[cosine, sines], [-sines, cosine]])
    return forward, forward.T


def by_owner(table, owners):
    two, kept, width = table.shape
    split = table.reshape(two, owners, kept // owners, width)
    return split.transpose(1, 0, 2, 3).reshape(two * kept, width)


def block_matrix(weights):
    _, blocks, size, _ = weights.shape
    real, imag = weights[0], weights[1]
    eye = jnp.eye(blocks, dtype=weights.dtype)

    def spread(w):
        full = eye[:, None, :, None] * w[:, :, None, :]
        return full.reshape(blocks * size, blocks * size)

    return jnp.block([[spread(real), spread(imag)], [spread(-imag), spread(real)]])


def params(steps):
    return pltpu.CompilerParams(vmem_limit_bytes=VMEM_LIMIT, dimension_semantics=("arbitrary",) * steps)


def cost(flops, nbytes, trans=0):
    return pl.CostEstimate(flops=int(flops), bytes_accessed=int(nbytes), transcendentals=int(trans))


def full_spec(shape):
    return pl.BlockSpec(shape, lambda i: (0,) * len(shape))


def row_forward(table, arrays, owners):
    h, n, c = arrays[0].shape
    pk = table.shape[0]
    hb = min(HBLOCK, h)
    count = len(arrays)

    def kernel(table_ref, *refs):
        ins, out_ref, held = refs[:count], refs[count], refs[count + 1]
        for j in range(hb):
            if count == 2:
                x = (ins[0][j].astype(jnp.float32) + ins[1][j].astype(jnp.float32)).astype(jnp.bfloat16)
            else:
                x = ins[0][j]
            held[j] = dot(table_ref[...], x)
        part = pk // owners
        for o in range(owners):
            piece = held[:, o * part : (o + 1) * part, :]
            out_ref[o] = jnp.swapaxes(piece, 0, 1).astype(jnp.bfloat16)

    return pl.pallas_call(
        kernel,
        grid=(h // hb,),
        in_specs=[full_spec(table.shape)] + [pl.BlockSpec((hb, n, c), lambda i: (i, 0, 0))] * count,
        out_specs=pl.BlockSpec((owners, pk // owners, hb, c), lambda i: (0, 0, i, 0)),
        out_shape=jax.ShapeDtypeStruct((owners, pk // owners, h, c), jnp.bfloat16),
        scratch_shapes=[pltpu.VMEM((hb, pk, c), jnp.float32)],
        compiler_params=params(1),
        cost_estimate=cost(2 * h * pk * n * c, 2 * h * n * c * (count + 1)),
        name="row_forward%d" % count,
    )(table, *arrays)


def row_inverse(table, spec, arrays, pieces):
    owners, part, h, c = spec.shape
    n, pk = table.shape
    hb = min(HBLOCK, h)
    count = len(arrays)
    wide = n // pieces

    def kernel(table_ref, spec_ref, *refs):
        ins, out_ref, held = refs[:count], refs[count], refs[count + 1]
        for o in range(owners):
            piece = spec_ref[o].astype(jnp.float32)
            held[:, o * part : (o + 1) * part, :] = jnp.swapaxes(piece, 0, 1)
        for j in range(hb):
            y = dot(table_ref[...], held[j].astype(jnp.bfloat16))
            if count == 2:
                x = ins[0][j].astype(jnp.float32) + ins[1][j].astype(jnp.float32)
                y = y + x.astype(jnp.bfloat16).astype(jnp.float32)
            elif count == 1:
                y = y + ins[0][j].astype(jnp.float32)
            for d in range(pieces):
                out_ref[d, j] = y[d * wide : (d + 1) * wide].astype(jnp.bfloat16)

    return pl.pallas_call(
        kernel,
        grid=(h // hb,),
        in_specs=[
            full_spec(table.shape),
            pl.BlockSpec((owners, part, hb, c), lambda i: (0, 0, i, 0)),
        ]
        + [pl.BlockSpec((hb, n, c), lambda i: (i, 0, 0))] * count,
        out_specs=pl.BlockSpec((pieces, hb, wide, c), lambda i: (0, i, 0, 0)),
        out_shape=jax.ShapeDtypeStruct((pieces, h, wide, c), jnp.bfloat16),
        scratch_shapes=[pltpu.VMEM((hb, pk, c), jnp.float32)],
        compiler_params=params(1),
        cost_estimate=cost(2 * h * pk * n * c, 2 * h * n * c * (count + 2)),
        name="row_inverse%d" % count,
    )(table, spec, *arrays)


def stacked(ref):
    owners, _, _, h, c = ref.shape
    return jnp.concatenate([ref[:, q, 0].reshape(owners * h, c) for q in range(2)], axis=0)


def beside(x):
    half = x.shape[0] // 2
    return jnp.concatenate([x[:half], x[half:]], axis=1)


def above(x):
    half = x.shape[1] // 2
    return jnp.concatenate([x[:, :half], x[:, half:]], axis=0)


def column_forward(spec, forward, inverse, first, second, first_bias, second_bias):
    owners, two, kept, h, c = spec.shape
    rows = owners * h

    def kernel(x_ref, f_ref, i_ref, m1_ref, m2_ref, b1_ref, b2_ref, out_ref, slope_ref):
        spectrum = dot(f_ref[...], stacked(x_ref)).astype(jnp.bfloat16)
        z = dot(beside(spectrum), m1_ref[...]) + b1_ref[...]
        cumulative = 0.5 * (1.0 + lax.erf(z * 0.7071067811865476))
        hidden = (z * cumulative).astype(jnp.bfloat16)
        slope_ref[0] = cumulative + z * (jnp.exp(-0.5 * z * z) * 0.3989422804014327)
        mixed = (dot(hidden, m2_ref[...]) + b2_ref[...]).astype(jnp.bfloat16)
        grid = dot(i_ref[...], above(mixed)).astype(jnp.bfloat16)
        for q in range(2):
            out_ref[:, q, 0] = grid[q * rows : (q + 1) * rows].reshape(owners, h, c)

    block = pl.BlockSpec((owners, two, 1, h, c), lambda i: (0, 0, i, 0, 0))
    return pl.pallas_call(
        kernel,
        grid=(kept,),
        in_specs=[block]
        + [full_spec(a.shape) for a in (forward, inverse, first, second, first_bias, second_bias)],
        out_specs=[block, pl.BlockSpec((1, rows, 2 * c), lambda i: (i, 0, 0))],
        out_shape=[
            jax.ShapeDtypeStruct(spec.shape, jnp.bfloat16),
            jax.ShapeDtypeStruct((kept, rows, 2 * c), jnp.float32),
        ],
        compiler_params=params(1),
        cost_estimate=cost(kept * (16 * rows * rows * c + 16 * rows * c * c), 16 * kept * rows * c, 4 * kept * rows * c),
        name="column_forward",
    )(spec, forward, inverse, first, second, first_bias, second_bias)


def column_backward(spec, slope, forward, first_t, second_t, inverse=None):
    owners, two, kept, h, c = spec.shape
    rows = owners * h
    extra = () if inverse is None else (inverse,)

    def kernel(x_ref, s_ref, f_ref, m1_ref, m2_ref, *refs):
        out_ref = refs[-1]
        back_out = dot(f_ref[...], stacked(x_ref)).astype(jnp.bfloat16)
        back_pre = (dot(beside(back_out), m2_ref[...]) * s_ref[0]).astype(jnp.bfloat16)
        back = above(dot(back_pre, m1_ref[...]).astype(jnp.bfloat16))
        if inverse is None:
            out_ref[0] = back
        else:
            grid = dot(refs[0][...], back).astype(jnp.bfloat16)
            for q in range(2):
                out_ref[:, q, 0] = grid[q * rows : (q + 1) * rows].reshape(owners, h, c)

    block = pl.BlockSpec((owners, two, 1, h, c), lambda i: (0, 0, i, 0, 0))
    flat = pl.BlockSpec((1, 2 * rows, c), lambda i: (i, 0, 0))
    return pl.pallas_call(
        kernel,
        grid=(kept,),
        in_specs=[block, pl.BlockSpec((1, rows, 2 * c), lambda i: (i, 0, 0))]
        + [full_spec(a.shape) for a in (forward, first_t, second_t) + extra],
        out_specs=flat if inverse is None else block,
        out_shape=jax.ShapeDtypeStruct((kept, 2 * rows, c) if inverse is None else spec.shape, jnp.bfloat16),
        compiler_params=params(1),
        cost_estimate=cost(kept * (8 * rows * rows * c + 16 * rows * c * c), 16 * kept * rows * c),
        name="column_backward",
    )(spec, slope, forward, first_t, second_t, *extra)


def column_summed(spec, inverse, owners, groups):
    kept, double, c = spec.shape
    rows = double // 2
    h = rows // owners // groups

    def kernel(x_ref, i_ref, out_ref):
        grid = dot(i_ref[...], x_ref[0])
        for q in range(2):
            part = grid[q * rows : (q + 1) * rows].reshape(owners, groups, h, c)
            for d in range(groups):
                out_ref[d, :, q, 0] = part[:, d].astype(jnp.bfloat16)

    return pl.pallas_call(
        kernel,
        grid=(kept,),
        in_specs=[pl.BlockSpec((1, double, c), lambda i: (i, 0, 0)), full_spec(inverse.shape)],
        out_specs=pl.BlockSpec((groups, owners, 2, 1, h, c), lambda i: (0, 0, 0, i, 0, 0)),
        out_shape=jax.ShapeDtypeStruct((groups, owners, 2, kept, h, c), jnp.bfloat16),
        compiler_params=params(1),
        cost_estimate=cost(kept * 8 * rows * rows * c, 8 * kept * rows * c),
        name="column_summed",
    )(spec, inverse)


def exchange(x, axis):
    return lax.all_to_all(x, axis, split_axis=0, concat_axis=0, tiled=True)


def on_device(groups, owners, scenes, prompt, cotangent, first_weight, first_bias, second_weight, second_bias):
    _, h, n, c = scenes.shape
    height = h * owners
    kept = n // 2
    own = kept // owners
    forward, inverse = row_tables(n, kept)
    fwd_rows, inv_rows = by_owner(forward, owners), by_owner(inverse, owners)
    column_fwd, column_inv = column_tables(height)
    first, second = block_matrix(first_weight), block_matrix(second_weight)
    scene, cot = scenes[0], cotangent[0]
    shape5 = (owners, 2, own, h, c)

    row_spec = row_forward(fwd_rows, [scene, prompt], owners)
    row_spec, cot_in = lax.optimization_barrier((row_spec, cot))
    row_cols = exchange(row_spec, "rows").reshape(shape5)
    back_spec = row_forward(inv_rows, [cot_in], owners)
    back_cols = exchange(back_spec, "rows").reshape(shape5)
    grid_cols, slope = column_forward(
        row_cols, column_fwd, column_inv, first, second, first_bias.reshape(1, -1), second_bias.reshape(1, -1)
    )
    grid_spec = exchange(grid_cols, "rows").reshape(owners, 2 * own, h, c)
    summable = own % groups == 0 and h % (8 * groups) == 0
    if summable:
        back = column_backward(back_cols, slope, column_fwd, first.T, second.T)
        total = lax.psum_scatter(back, "dp", scatter_dimension=0, tiled=True)
        cot_total = lax.psum_scatter(cot, "dp", scatter_dimension=1, tiled=True)
        grad_cols = column_summed(total, column_inv, owners, groups)
        few, low = own // groups, h // groups
        back_rows = exchange(grad_cols.reshape(groups * owners, 2 * few, low, c), ("dp", "rows"))
        table = forward.reshape(2, owners, groups, few, n).transpose(4, 2, 1, 0, 3).reshape(n, 2 * kept)
        grad = row_inverse(table, back_rows, [], groups)
        grad = exchange(grad, "dp").reshape(h, n // groups, c)
        prompt_grad = cot_total.astype(jnp.float32) + grad.astype(jnp.float32)
    else:
        grad_cols = column_backward(back_cols, slope, column_fwd, first.T, second.T, column_inv)
        back_rows = exchange(grad_cols, "rows").reshape(owners, 2 * own, h, c)
        local = row_inverse(fwd_rows.T, back_rows, [cot], 1)[0]
        prompt_grad = lax.psum_scatter(local, "dp", scatter_dimension=1, tiled=True).astype(jnp.float32)
    mixed = row_inverse(inv_rows.T, grid_spec, [scene, prompt], 1)
    return mixed, prompt_grad


def solution(mesh):
    return jax.shard_map(
        functools.partial(on_device, mesh.shape["dp"], mesh.shape["rows"]),
        mesh=mesh,
        in_specs=(
            P("dp", "rows", None, None),
            P("rows", None, None),
            P("dp", "rows", None, None),
            P(),
            P(),
            P(),
            P(),
        ),
        out_specs=(P("dp", "rows", None, None), P("rows", "dp", None)),
        check_vma=False,
    )
```

```python
import functools
import math

import jax
import jax.numpy as jnp
from jax import lax
from jax.experimental import pallas as pl
from jax.experimental.pallas import tpu as pltpu
from jax.sharding import PartitionSpec as P

VMEM_LIMIT = 48 * 1024 * 1024
HBLOCK = 16


def dot(left, right):
    return jnp.dot(left, right, preferred_element_type=jnp.float32)


def row_tables(width, kept):
    grid_index = jnp.arange(width, dtype=jnp.int32)
    mode_index = jnp.arange(kept, dtype=jnp.int32)
    phases = mode_index[:, None] * grid_index[None, :] % width
    angles = phases.astype(jnp.float32) * (2.0 * math.pi / width)
    factor = 1.0 / math.sqrt(width)
    cosine = jnp.cos(angles) * factor
    sines = jnp.sin(angles) * factor
    forward = jnp.stack([cosine, -sines], axis=0).astype(jnp.bfloat16)
    doubled = jnp.where(mode_index == 0, 1.0, 2.0).astype(jnp.float32)[:, None]
    inverse = jnp.stack([doubled * cosine, -doubled * sines], axis=0).astype(jnp.bfloat16)
    return forward, inverse


def column_tables(height):
    grid_index = jnp.arange(height, dtype=jnp.int32)
    phases = grid_index[:, None] * grid_index[None, :] % height
    angles = phases.astype(jnp.float32) * (2.0 * math.pi / height)
    factor = 1.0 / math.sqrt(height)
    cosine = (jnp.cos(angles) * factor).astype(jnp.bfloat16)
    sines = (jnp.sin(angles) * factor).astype(jnp.bfloat16)
    forward = jnp.block([[cosine, sines], [-sines, cosine]])
    return forward, forward.T


def by_owner(table, owners):
    two, kept, width = table.shape
    split = table.reshape(two, owners, kept // owners, width)
    return split.transpose(1, 0, 2, 3).reshape(two * kept, width)


def block_matrix(weights):
    _, blocks, size, _ = weights.shape
    real, imag = weights[0], weights[1]
    eye = jnp.eye(blocks, dtype=weights.dtype)

    def spread(w):
        full = eye[:, None, :, None] * w[:, :, None, :]
        return full.reshape(blocks * size, blocks * size)

    return jnp.block([[spread(real), spread(imag)], [spread(-imag), spread(real)]])


def params(steps):
    return pltpu.CompilerParams(vmem_limit_bytes=VMEM_LIMIT, dimension_semantics=("arbitrary",) * steps)


def cost(flops, nbytes, trans=0):
    return pl.CostEstimate(flops=int(flops), bytes_accessed=int(nbytes), transcendentals=int(trans))


def full_spec(shape):
    return pl.BlockSpec(shape, lambda i: (0,) * len(shape))


def row_forward(table, arrays, owners):
    h, n, c = arrays[0].shape
    pk = table.shape[0]
    hb = min(HBLOCK, h)
    count = len(arrays)

    def kernel(table_ref, *refs):
        ins, out_ref, held = refs[:count], refs[count], refs[count + 1]
        for j in range(hb):
            if count == 2:
                x = (ins[0][j].astype(jnp.float32) + ins[1][j].astype(jnp.float32)).astype(jnp.bfloat16)
            else:
                x = ins[0][j]
            held[j] = dot(table_ref[...], x)
        part = pk // owners
        for o in range(owners):
            piece = held[:, o * part : (o + 1) * part, :]
            out_ref[o] = jnp.swapaxes(piece, 0, 1).astype(jnp.bfloat16)

    return pl.pallas_call(
        kernel,
        grid=(h // hb,),
        in_specs=[full_spec(table.shape)] + [pl.BlockSpec((hb, n, c), lambda i: (i, 0, 0))] * count,
        out_specs=pl.BlockSpec((owners, pk // owners, hb, c), lambda i: (0, 0, i, 0)),
        out_shape=jax.ShapeDtypeStruct((owners, pk // owners, h, c), jnp.bfloat16),
        scratch_shapes=[pltpu.VMEM((hb, pk, c), jnp.float32)],
        compiler_params=params(1),
        cost_estimate=cost(2 * h * pk * n * c, 2 * h * n * c * (count + 1)),
        name="row_forward%d" % count,
    )(table, *arrays)


def row_inverse(table, spec, arrays, pieces):
    owners, part, h, c = spec.shape
    n, pk = table.shape
    hb = min(HBLOCK, h)
    count = len(arrays)
    wide = n // pieces

    def kernel(table_ref, spec_ref, *refs):
        ins, out_ref, held = refs[:count], refs[count], refs[count + 1]
        for o in range(owners):
            piece = spec_ref[o].astype(jnp.float32)
            held[:, o * part : (o + 1) * part, :] = jnp.swapaxes(piece, 0, 1)
        for j in range(hb):
            y = dot(table_ref[...], held[j].astype(jnp.bfloat16))
            if count == 2:
                x = ins[0][j].astype(jnp.float32) + ins[1][j].astype(jnp.float32)
                y = y + x.astype(jnp.bfloat16).astype(jnp.float32)
            elif count == 1:
                y = y + ins[0][j].astype(jnp.float32)
            for d in range(pieces):
                out_ref[d, j] = y[d * wide : (d + 1) * wide].astype(jnp.bfloat16)

    return pl.pallas_call(
        kernel,
        grid=(h // hb,),
        in_specs=[
            full_spec(table.shape),
            pl.BlockSpec((owners, part, hb, c), lambda i: (0, 0, i, 0)),
        ]
        + [pl.BlockSpec((hb, n, c), lambda i: (i, 0, 0))] * count,
        out_specs=pl.BlockSpec((pieces, hb, wide, c), lambda i: (0, i, 0, 0)),
        out_shape=jax.ShapeDtypeStruct((pieces, h, wide, c), jnp.bfloat16),
        scratch_shapes=[pltpu.VMEM((hb, pk, c), jnp.float32)],
        compiler_params=params(1),
        cost_estimate=cost(2 * h * pk * n * c, 2 * h * n * c * (count + 2)),
        name="row_inverse%d" % count,
    )(table, spec, *arrays)


def stacked(ref):
    owners, _, _, h, c = ref.shape
    return jnp.concatenate([ref[:, q, 0].reshape(owners * h, c) for q in range(2)], axis=0)


def beside(x):
    half = x.shape[0] // 2
    return jnp.concatenate([x[:half], x[half:]], axis=1)


def above(x):
    half = x.shape[1] // 2
    return jnp.concatenate([x[:, :half], x[:, half:]], axis=0)


def column_forward(spec, forward, inverse, first, second, first_bias, second_bias):
    owners, two, kept, h, c = spec.shape
    rows = owners * h

    def kernel(x_ref, f_ref, i_ref, m1_ref, m2_ref, b1_ref, b2_ref, out_ref, slope_ref):
        spectrum = dot(f_ref[...], stacked(x_ref)).astype(jnp.bfloat16)
        z = dot(beside(spectrum), m1_ref[...]) + b1_ref[...]
        cumulative = 0.5 * (1.0 + lax.erf(z * 0.7071067811865476))
        hidden = (z * cumulative).astype(jnp.bfloat16)
        slope_ref[0] = cumulative + z * (jnp.exp(-0.5 * z * z) * 0.3989422804014327)
        mixed = (dot(hidden, m2_ref[...]) + b2_ref[...]).astype(jnp.bfloat16)
        grid = dot(i_ref[...], above(mixed)).astype(jnp.bfloat16)
        for q in range(2):
            out_ref[:, q, 0] = grid[q * rows : (q + 1) * rows].reshape(owners, h, c)

    block = pl.BlockSpec((owners, two, 1, h, c), lambda i: (0, 0, i, 0, 0))
    return pl.pallas_call(
        kernel,
        grid=(kept,),
        in_specs=[block]
        + [full_spec(a.shape) for a in (forward, inverse, first, second, first_bias, second_bias)],
        out_specs=[block, pl.BlockSpec((1, rows, 2 * c), lambda i: (i, 0, 0))],
        out_shape=[
            jax.ShapeDtypeStruct(spec.shape, jnp.bfloat16),
            jax.ShapeDtypeStruct((kept, rows, 2 * c), jnp.float32),
        ],
        compiler_params=params(1),
        cost_estimate=cost(kept * (16 * rows * rows * c + 16 * rows * c * c), 16 * kept * rows * c, 4 * kept * rows * c),
        name="column_forward",
    )(spec, forward, inverse, first, second, first_bias, second_bias)


def column_backward(spec, slope, forward, first_t, second_t, inverse=None):
    owners, two, kept, h, c = spec.shape
    rows = owners * h
    extra = () if inverse is None else (inverse,)

    def kernel(x_ref, s_ref, f_ref, m1_ref, m2_ref, *refs):
        out_ref = refs[-1]
        back_out = dot(f_ref[...], stacked(x_ref)).astype(jnp.bfloat16)
        back_pre = (dot(beside(back_out), m2_ref[...]) * s_ref[0]).astype(jnp.bfloat16)
        back = above(dot(back_pre, m1_ref[...]).astype(jnp.bfloat16))
        if inverse is None:
            out_ref[0] = back
        else:
            grid = dot(refs[0][...], back).astype(jnp.bfloat16)
            for q in range(2):
                out_ref[:, q, 0] = grid[q * rows : (q + 1) * rows].reshape(owners, h, c)

    block = pl.BlockSpec((owners, two, 1, h, c), lambda i: (0, 0, i, 0, 0))
    flat = pl.BlockSpec((1, 2 * rows, c), lambda i: (i, 0, 0))
    return pl.pallas_call(
        kernel,
        grid=(kept,),
        in_specs=[block, pl.BlockSpec((1, rows, 2 * c), lambda i: (i, 0, 0))]
        + [full_spec(a.shape) for a in (forward, first_t, second_t) + extra],
        out_specs=flat if inverse is None else block,
        out_shape=jax.ShapeDtypeStruct((kept, 2 * rows, c) if inverse is None else spec.shape, jnp.bfloat16),
        compiler_params=params(1),
        cost_estimate=cost(kept * (8 * rows * rows * c + 16 * rows * c * c), 16 * kept * rows * c),
        name="column_backward",
    )(spec, slope, forward, first_t, second_t, *extra)


def column_summed(spec, inverse, owners, groups):
    kept, double, c = spec.shape
    rows = double // 2
    h = rows // owners // groups

    def kernel(x_ref, i_ref, out_ref):
        grid = dot(i_ref[...], x_ref[0])
        for q in range(2):
            part = grid[q * rows : (q + 1) * rows].reshape(owners, groups, h, c)
            for d in range(groups):
                out_ref[d, :, q, 0] = part[:, d].astype(jnp.bfloat16)

    return pl.pallas_call(
        kernel,
        grid=(kept,),
        in_specs=[pl.BlockSpec((1, double, c), lambda i: (i, 0, 0)), full_spec(inverse.shape)],
        out_specs=pl.BlockSpec((groups, owners, 2, 1, h, c), lambda i: (0, 0, 0, i, 0, 0)),
        out_shape=jax.ShapeDtypeStruct((groups, owners, 2, kept, h, c), jnp.bfloat16),
        compiler_params=params(1),
        cost_estimate=cost(kept * 8 * rows * rows * c, 8 * kept * rows * c),
        name="column_summed",
    )(spec, inverse)


def exchange(x, axis):
    return lax.all_to_all(x, axis, split_axis=0, concat_axis=0, tiled=True)


def on_device(groups, owners, scenes, prompt, cotangent, first_weight, first_bias, second_weight, second_bias):
    _, h, n, c = scenes.shape
    height = h * owners
    kept = n // 2
    own = kept // owners
    forward, inverse = row_tables(n, kept)
    fwd_rows, inv_rows = by_owner(forward, owners), by_owner(inverse, owners)
    column_fwd, column_inv = column_tables(height)
    first, second = block_matrix(first_weight), block_matrix(second_weight)
    scene, cot = scenes[0], cotangent[0]
    shape5 = (owners, 2, own, h, c)

    row_spec = row_forward(fwd_rows, [scene, prompt], owners)
    row_spec, cot_in = lax.optimization_barrier((row_spec, cot))
    row_cols = exchange(row_spec, "rows").reshape(shape5)
    back_spec = row_forward(inv_rows, [cot_in], owners)
    back_cols = exchange(back_spec, "rows").reshape(shape5)
    grid_cols, slope = column_forward(
        row_cols, column_fwd, column_inv, first, second, first_bias.reshape(1, -1), second_bias.reshape(1, -1)
    )
    grid_spec = exchange(grid_cols, "rows").reshape(owners, 2 * own, h, c)
    summable = own % groups == 0 and h % (8 * groups) == 0
    if summable:
        cot_total = lax.psum_scatter(cot, "dp", scatter_dimension=1, tiled=True)
        back_cols, cot_total = lax.optimization_barrier((back_cols, cot_total))
        back = column_backward(back_cols, slope, column_fwd, first.T, second.T)
        total = lax.psum_scatter(back, "dp", scatter_dimension=0, tiled=True)
        grad_cols = column_summed(total, column_inv, owners, groups)
        grad_cols, grid_spec = lax.optimization_barrier((grad_cols, grid_spec))
        few, low = own // groups, h // groups
        back_rows = exchange(grad_cols.reshape(groups * owners, 2 * few, low, c), ("dp", "rows"))
        table = forward.reshape(2, owners, groups, few, n).transpose(4, 2, 1, 0, 3).reshape(n, 2 * kept)
        grad = row_inverse(table, back_rows, [], groups)
        grad = exchange(grad, "dp").reshape(h, n // groups, c)
        prompt_grad = cot_total.astype(jnp.float32) + grad.astype(jnp.float32)
    else:
        grad_cols = column_backward(back_cols, slope, column_fwd, first.T, second.T, column_inv)
        back_rows = exchange(grad_cols, "rows").reshape(owners, 2 * own, h, c)
        local = row_inverse(fwd_rows.T, back_rows, [cot], 1)[0]
        prompt_grad = lax.psum_scatter(local, "dp", scatter_dimension=1, tiled=True).astype(jnp.float32)
    mixed = row_inverse(inv_rows.T, grid_spec, [scene, prompt], 1)
    return mixed, prompt_grad


def solution(mesh):
    return jax.shard_map(
        functools.partial(on_device, mesh.shape["dp"], mesh.shape["rows"]),
        mesh=mesh,
        in_specs=(
            P("dp", "rows", None, None),
            P("rows", None, None),
            P("dp", "rows", None, None),
            P(),
            P(),
            P(),
            P(),
        ),
        out_specs=(P("dp", "rows", None, None), P("rows", "dp", None)),
        check_vma=False,
    )
```

```python
import functools
import math

import jax
import jax.numpy as jnp
from jax import lax
from jax.experimental import pallas as pl
from jax.experimental.pallas import tpu as pltpu
from jax.sharding import PartitionSpec as P

VMEM_LIMIT = 48 * 1024 * 1024
HBLOCK = 16


def dot(left, right):
    return jnp.dot(left, right, preferred_element_type=jnp.float32)


def row_tables(width, kept):
    grid_index = jnp.arange(width, dtype=jnp.int32)
    mode_index = jnp.arange(kept, dtype=jnp.int32)
    phases = mode_index[:, None] * grid_index[None, :] % width
    angles = phases.astype(jnp.float32) * (2.0 * math.pi / width)
    factor = 1.0 / math.sqrt(width)
    cosine = jnp.cos(angles) * factor
    sines = jnp.sin(angles) * factor
    forward = jnp.stack([cosine, -sines], axis=0).astype(jnp.bfloat16)
    doubled = jnp.where(mode_index == 0, 1.0, 2.0).astype(jnp.float32)[:, None]
    inverse = jnp.stack([doubled * cosine, -doubled * sines], axis=0).astype(jnp.bfloat16)
    return forward, inverse


def column_tables(height):
    grid_index = jnp.arange(height, dtype=jnp.int32)
    phases = grid_index[:, None] * grid_index[None, :] % height
    angles = phases.astype(jnp.float32) * (2.0 * math.pi / height)
    factor = 1.0 / math.sqrt(height)
    cosine = (jnp.cos(angles) * factor).astype(jnp.bfloat16)
    sines = (jnp.sin(angles) * factor).astype(jnp.bfloat16)
    forward = jnp.block([[cosine, sines], [-sines, cosine]])
    return forward, forward.T


def by_owner(table, owners):
    two, kept, width = table.shape
    split = table.reshape(two, owners, kept // owners, width)
    return split.transpose(1, 0, 2, 3).reshape(two * kept, width)


def block_matrix(weights):
    _, blocks, size, _ = weights.shape
    real, imag = weights[0], weights[1]
    eye = jnp.eye(blocks, dtype=weights.dtype)

    def spread(w):
        full = eye[:, None, :, None] * w[:, :, None, :]
        return full.reshape(blocks * size, blocks * size)

    return jnp.block([[spread(real), spread(imag)], [spread(-imag), spread(real)]])


def params(steps):
    return pltpu.CompilerParams(vmem_limit_bytes=VMEM_LIMIT, dimension_semantics=("arbitrary",) * steps)


def cost(flops, nbytes, trans=0):
    return pl.CostEstimate(flops=int(flops), bytes_accessed=int(nbytes), transcendentals=int(trans))


def full_spec(shape):
    return pl.BlockSpec(shape, lambda i: (0,) * len(shape))


def spans(widths):
    ends = [sum(widths[: i + 1]) for i in range(len(widths))]
    return list(zip([0] + ends[:-1], ends))


def row_forward(table, arrays, owners):
    h, n, c = arrays[0].shape
    pk = table.shape[0]
    hb = min(HBLOCK, h)
    count = len(arrays)

    def kernel(table_ref, *refs):
        ins, out_ref, held = refs[:count], refs[count], refs[count + 1]
        for j in range(hb):
            if count == 2:
                x = (ins[0][j].astype(jnp.float32) + ins[1][j].astype(jnp.float32)).astype(jnp.bfloat16)
            else:
                x = ins[0][j]
            held[j] = dot(table_ref[...], x)
        part = pk // owners
        for o in range(owners):
            piece = held[:, o * part : (o + 1) * part, :]
            out_ref[o] = jnp.swapaxes(piece, 0, 1).astype(jnp.bfloat16)

    return pl.pallas_call(
        kernel,
        grid=(h // hb,),
        in_specs=[full_spec(table.shape)] + [pl.BlockSpec((hb, n, c), lambda i: (i, 0, 0))] * count,
        out_specs=pl.BlockSpec((owners, pk // owners, hb, c), lambda i: (0, 0, i, 0)),
        out_shape=jax.ShapeDtypeStruct((owners, pk // owners, h, c), jnp.bfloat16),
        scratch_shapes=[pltpu.VMEM((hb, pk, c), jnp.float32)],
        compiler_params=params(1),
        cost_estimate=cost(2 * h * pk * n * c, 2 * h * n * c * (count + 1)),
        name="row_forward%d" % count,
    )(table, *arrays)


def row_inverse(table, specs, arrays, pieces):
    owners, part, h, _ = specs[0].shape
    lanes = spans([spec.shape[-1] for spec in specs])
    c = lanes[-1][1]
    cut = len(specs)
    n, pk = table.shape
    hb = min(HBLOCK, h)
    count = len(arrays)
    wide = n // pieces

    def kernel(table_ref, *refs):
        spec_refs, refs = refs[:cut], refs[cut:]
        ins, out_ref, held = refs[:count], refs[count], refs[count + 1]
        for spec_ref, (low, high) in zip(spec_refs, lanes):
            for o in range(owners):
                piece = spec_ref[o].astype(jnp.float32)
                held[:, o * part : (o + 1) * part, low:high] = jnp.swapaxes(piece, 0, 1)
        for j in range(hb):
            y = dot(table_ref[...], held[j].astype(jnp.bfloat16))
            if count == 2:
                x = ins[0][j].astype(jnp.float32) + ins[1][j].astype(jnp.float32)
                y = y + x.astype(jnp.bfloat16).astype(jnp.float32)
            elif count == 1:
                y = y + ins[0][j].astype(jnp.float32)
            for d in range(pieces):
                out_ref[d, j] = y[d * wide : (d + 1) * wide].astype(jnp.bfloat16)

    return pl.pallas_call(
        kernel,
        grid=(h // hb,),
        in_specs=[full_spec(table.shape)]
        + [pl.BlockSpec((owners, part, hb, high - low), lambda i: (0, 0, i, 0)) for low, high in lanes]
        + [pl.BlockSpec((hb, n, c), lambda i: (i, 0, 0))] * count,
        out_specs=pl.BlockSpec((pieces, hb, wide, c), lambda i: (0, i, 0, 0)),
        out_shape=jax.ShapeDtypeStruct((pieces, h, wide, c), jnp.bfloat16),
        scratch_shapes=[pltpu.VMEM((hb, pk, c), jnp.float32)],
        compiler_params=params(1),
        cost_estimate=cost(2 * h * pk * n * c, 2 * h * n * c * (count + 2)),
        name="row_inverse%d" % count,
    )(table, *specs, *arrays)


def stacked(ref):
    owners, _, _, h, c = ref.shape
    return jnp.concatenate([ref[:, q, 0].reshape(owners * h, c) for q in range(2)], axis=0)


def beside(x):
    half = x.shape[0] // 2
    return jnp.concatenate([x[:half], x[half:]], axis=1)


def above(x):
    half = x.shape[1] // 2
    return jnp.concatenate([x[:, :half], x[:, half:]], axis=0)


def column_forward(spec, forward, inverse, first, second, first_bias, second_bias, widths):
    owners, two, kept, h, c = spec.shape
    lanes = spans(widths)
    rows = owners * h

    def kernel(x_ref, f_ref, i_ref, m1_ref, m2_ref, b1_ref, b2_ref, *out_refs):
        slope_ref = out_refs[-1]
        spectrum = dot(f_ref[...], stacked(x_ref)).astype(jnp.bfloat16)
        z = dot(beside(spectrum), m1_ref[...]) + b1_ref[...]
        cumulative = 0.5 * (1.0 + lax.erf(z * 0.7071067811865476))
        hidden = (z * cumulative).astype(jnp.bfloat16)
        slope_ref[0] = cumulative + z * (jnp.exp(-0.5 * z * z) * 0.3989422804014327)
        mixed = (dot(hidden, m2_ref[...]) + b2_ref[...]).astype(jnp.bfloat16)
        grid = dot(i_ref[...], above(mixed)).astype(jnp.bfloat16)
        for out_ref, (low, high) in zip(out_refs, lanes):
            for q in range(2):
                piece = grid[q * rows : (q + 1) * rows, low:high]
                out_ref[:, q, 0] = piece.reshape(owners, h, high - low)

    block = pl.BlockSpec((owners, two, 1, h, c), lambda i: (0, 0, i, 0, 0))
    outs = [pl.BlockSpec((owners, two, 1, h, w), lambda i: (0, 0, i, 0, 0)) for w in widths]
    return pl.pallas_call(
        kernel,
        grid=(kept,),
        in_specs=[block]
        + [full_spec(a.shape) for a in (forward, inverse, first, second, first_bias, second_bias)],
        out_specs=outs + [pl.BlockSpec((1, rows, 2 * c), lambda i: (i, 0, 0))],
        out_shape=[jax.ShapeDtypeStruct((owners, two, kept, h, w), jnp.bfloat16) for w in widths]
        + [jax.ShapeDtypeStruct((kept, rows, 2 * c), jnp.float32)],
        compiler_params=params(1),
        cost_estimate=cost(kept * (16 * rows * rows * c + 16 * rows * c * c), 16 * kept * rows * c, 4 * kept * rows * c),
        name="column_forward",
    )(spec, forward, inverse, first, second, first_bias, second_bias)


def column_backward(spec, slope, forward, first_t, second_t, inverse=None):
    owners, two, kept, h, c = spec.shape
    rows = owners * h
    extra = () if inverse is None else (inverse,)

    def kernel(x_ref, s_ref, f_ref, m1_ref, m2_ref, *refs):
        out_ref = refs[-1]
        back_out = dot(f_ref[...], stacked(x_ref)).astype(jnp.bfloat16)
        back_pre = (dot(beside(back_out), m2_ref[...]) * s_ref[0]).astype(jnp.bfloat16)
        back = above(dot(back_pre, m1_ref[...]).astype(jnp.bfloat16))
        if inverse is None:
            out_ref[0] = back
        else:
            grid = dot(refs[0][...], back).astype(jnp.bfloat16)
            for q in range(2):
                out_ref[:, q, 0] = grid[q * rows : (q + 1) * rows].reshape(owners, h, c)

    block = pl.BlockSpec((owners, two, 1, h, c), lambda i: (0, 0, i, 0, 0))
    flat = pl.BlockSpec((1, 2 * rows, c), lambda i: (i, 0, 0))
    return pl.pallas_call(
        kernel,
        grid=(kept,),
        in_specs=[block, pl.BlockSpec((1, rows, 2 * c), lambda i: (i, 0, 0))]
        + [full_spec(a.shape) for a in (forward, first_t, second_t) + extra],
        out_specs=flat if inverse is None else block,
        out_shape=jax.ShapeDtypeStruct((kept, 2 * rows, c) if inverse is None else spec.shape, jnp.bfloat16),
        compiler_params=params(1),
        cost_estimate=cost(kept * (8 * rows * rows * c + 16 * rows * c * c), 16 * kept * rows * c),
        name="column_backward",
    )(spec, slope, forward, first_t, second_t, *extra)


def column_summed(spec, inverse, owners, groups):
    kept, double, c = spec.shape
    rows = double // 2
    h = rows // owners // groups

    def kernel(x_ref, i_ref, out_ref):
        grid = dot(i_ref[...], x_ref[0])
        for q in range(2):
            part = grid[q * rows : (q + 1) * rows].reshape(owners, groups, h, c)
            for d in range(groups):
                out_ref[d, :, q, 0] = part[:, d].astype(jnp.bfloat16)

    return pl.pallas_call(
        kernel,
        grid=(kept,),
        in_specs=[pl.BlockSpec((1, double, c), lambda i: (i, 0, 0)), full_spec(inverse.shape)],
        out_specs=pl.BlockSpec((groups, owners, 2, 1, h, c), lambda i: (0, 0, 0, i, 0, 0)),
        out_shape=jax.ShapeDtypeStruct((groups, owners, 2, kept, h, c), jnp.bfloat16),
        compiler_params=params(1),
        cost_estimate=cost(kept * 8 * rows * rows * c, 8 * kept * rows * c),
        name="column_summed",
    )(spec, inverse)


def exchange(x, axis):
    return lax.all_to_all(x, axis, split_axis=0, concat_axis=0, tiled=True)


def on_device(groups, owners, scenes, prompt, cotangent, first_weight, first_bias, second_weight, second_bias):
    _, h, n, c = scenes.shape
    height = h * owners
    kept = n // 2
    own = kept // owners
    forward, inverse = row_tables(n, kept)
    fwd_rows, inv_rows = by_owner(forward, owners), by_owner(inverse, owners)
    column_fwd, column_inv = column_tables(height)
    first, second = block_matrix(first_weight), block_matrix(second_weight)
    scene, cot = scenes[0], cotangent[0]
    shape5 = (owners, 2, own, h, c)

    row_spec = row_forward(fwd_rows, [scene, prompt], owners)
    row_spec, cot_in = lax.optimization_barrier((row_spec, cot))
    row_cols = exchange(row_spec, "rows").reshape(shape5)
    back_spec = row_forward(inv_rows, [cot_in], owners)
    back_cols = exchange(back_spec, "rows").reshape(shape5)
    lead = 128 if c > 128 else c // 2
    biases = first_bias.reshape(1, -1), second_bias.reshape(1, -1)
    lead_cols, rest_cols, slope = column_forward(
        row_cols, column_fwd, column_inv, first, second, *biases, (lead, c - lead)
    )
    grid_lead = exchange(lead_cols, "rows")
    summable = own % groups == 0 and h % (8 * groups) == 0
    if summable:
        cot_total = lax.psum_scatter(cot, "dp", scatter_dimension=1, tiled=True)
        back_cols, cot_total = lax.optimization_barrier((back_cols, cot_total))
        back = column_backward(back_cols, slope, column_fwd, first.T, second.T)
        rest_cols, grid_lead, back = lax.optimization_barrier((rest_cols, grid_lead, back))
        grid_rest = exchange(rest_cols, "rows")
        total = lax.psum_scatter(back, "dp", scatter_dimension=0, tiled=True)
        grad_cols = column_summed(total, column_inv, owners, groups)
        grad_cols, grid_rest = lax.optimization_barrier((grad_cols, grid_rest))
        few, low = own // groups, h // groups
        back_rows = exchange(grad_cols.reshape(groups * owners, 2 * few, low, c), ("dp", "rows"))
        table = forward.reshape(2, owners, groups, few, n).transpose(4, 2, 1, 0, 3).reshape(n, 2 * kept)
        grad = row_inverse(table, [back_rows], [], groups)
        grad = exchange(grad, "dp").reshape(h, n // groups, c)
        prompt_grad = cot_total.astype(jnp.float32) + grad.astype(jnp.float32)
    else:
        grid_rest = exchange(rest_cols, "rows")
        grad_cols = column_backward(back_cols, slope, column_fwd, first.T, second.T, column_inv)
        back_rows = exchange(grad_cols, "rows").reshape(owners, 2 * own, h, c)
        local = row_inverse(fwd_rows.T, [back_rows], [cot], 1)[0]
        prompt_grad = lax.psum_scatter(local, "dp", scatter_dimension=1, tiled=True).astype(jnp.float32)
    grid_spec = [part.reshape(owners, 2 * own, h, part.shape[-1]) for part in (grid_lead, grid_rest)]
    mixed = row_inverse(inv_rows.T, grid_spec, [scene, prompt], 1)
    return mixed, prompt_grad


def solution(mesh):
    return jax.shard_map(
        functools.partial(on_device, mesh.shape["dp"], mesh.shape["rows"]),
        mesh=mesh,
        in_specs=(
            P("dp", "rows", None, None),
            P("rows", None, None),
            P("dp", "rows", None, None),
            P(),
            P(),
            P(),
            P(),
        ),
        out_specs=(P("dp", "rows", None, None), P("rows", "dp", None)),
        check_vma=False,
    )
```
